32 devices in a mesh: grp: 2 (over y), slab: 4 (over z), mem: 2 (over x), sub: 2 (over core).
Axes of the slice: x: 2, y: 2, z: 4, core: 2. Of those that a mesh axis runs over, the one named last changes fastest.
Arguments:
- state: bfloat16 [256, 32768], P('mem', ('grp', 'slab', 'sub')), parts along dimension 1, may hold values from -6 to 6
- centers: int32 [512], P('grp'), parts along dimension 0, may hold values from 0 to 16383, as said below
- half_width: int32 [512], P('grp'), parts along dimension 0, may hold values from 4 to 71
- radius: int32 [512], P('grp'), parts along dimension 0, may hold values from 2048 to 8192
- order: int32 [512], P('grp'), parts along dimension 0, may hold values from 0 to 255, each once
- obs_var: float32 [512], P('grp'), parts along dimension 0, may hold values from 0.1 to 1
Outputs:
- analysis: bfloat16 [256, 32768], P('mem', ('grp', 'slab', 'sub')), parts along dimension 1
The draws below stay inside these ranges and needn't reach their ends.
There are 2 independent parts, one for each index of `grp`. The reference program is written for one: setup_inputs(seed, part) draws one part's arguments, and reference() takes and returns one part's arrays. A program takes and returns all parts, laid end to end along the dimension named above; each array names one. Nothing has to cross between parts.
Inputs may be any that keep to these rules, and one draw needn't show every extreme that they name: order holds every observation number once. Observations 4 k to 4 k + 3 have centers within 6 rows of a common site row, which the first of them sits on; centers are clipped to the grid.
All inputs are finite; a program needn't handle non-finite values.
Results may differ from the reference program's by a relative error of at most 0.0049.
Values may be sent and summed in bfloat16 or wider, within the bound.
A program may use at most 64 MiB of HBM per device.

```python
import math
import jax
import jax.numpy as jnp
from jax import lax

M = 256
P_SIZE = 128
BATCHES = 2
ROWS_DEV = 2048
NROWS = 16384
NOBS = 256


def draw_centers(key, part):
    site_key = jax.random.fold_in(key, 11)
    jitter_key = jax.random.fold_in(key, 12)
    site_count = NOBS // 4
    site_rows = jax.random.randint(site_key, (site_count,), 0, NROWS)
    slot_index = lax.iota(jnp.int32, site_count)
    site_rows = jnp.where(slot_index == 0, 0, jnp.where(slot_index == 1, NROWS - 1, site_rows))
    spread = ROWS_DEV // 512 + 2
    jitter = jax.random.randint(jitter_key, (NOBS,), -spread, spread + 1)
    obs_index = lax.iota(jnp.int32, NOBS)
    jitter = jnp.where(obs_index % 4 == 0, 0, jitter)
    centers = jnp.repeat(site_rows, 4) + jitter
    return jnp.clip(centers, 0, NROWS - 1).astype(jnp.int32)


def place_ends(result, stream_key, smallest, high):
    longest = result.shape.index(max(result.shape))
    spots = []
    for shift in (0, 1):
        where = [jax.random.randint(jax.random.fold_in(stream_key, axis), (), 0, length) for axis, length in enumerate(result.shape)]
        where[longest] = (where[longest] + shift) % result.shape[longest]
        spots.append(tuple(where))
    return result.at[spots[0]].set(smallest).at[spots[1]].set(high)


def block_scale(key, shape, shards, least, high):
    def one(position, shards_of):
        heights = jax.random.uniform(jax.random.fold_in(jax.random.fold_in(key, 6), position), (shards_of,), jnp.float32, least / len(shards), high / len(shards))
        return jnp.repeat(jnp.exp(heights), shape[position] // shards_of).reshape((-1,) + (1,) * (len(shape) - position - 1))

    gain = one(*shards[0])
    for cut in shards[1:]:
        gain = gain * one(*cut)
    return gain


def gaussian(key, dims, deviation, reach, split=(), kind=jnp.bfloat16):
    drawn = deviation * jax.random.normal(key, dims, jnp.float32)
    if split:
        drawn = drawn * block_scale(key, dims, split, -0.22, 0.18)
    return jnp.clip(drawn, -reach, reach).astype(kind)


def setup_inputs(seed: int = 0, part: int = 0) -> dict:
    keys = jax.random.split(jax.random.key(seed), 7)
    own_keys = jax.random.split(jax.random.fold_in(keys[6], part), 7)
    state = gaussian(own_keys[0], (M, NROWS), 1.0, 6.0, ((0, 2), (1, 8)))
    centers = draw_centers(jax.random.fold_in(jax.random.fold_in(keys[6], part), 71), part)
    half_width = place_ends(jax.random.randint(own_keys[2], (NOBS,), 4, ROWS_DEV // 32 + 8), jax.random.fold_in(own_keys[2], 1), 4, (ROWS_DEV // 32 + 8) - 1).astype(jnp.int32)
    radius = place_ends(jax.random.randint(own_keys[3], (NOBS,), ROWS_DEV, 4 * ROWS_DEV + 1), jax.random.fold_in(own_keys[3], 1), ROWS_DEV, 4 * ROWS_DEV).astype(jnp.int32)
    order = jax.random.permutation(own_keys[4], NOBS).astype(jnp.int32)
    obs_var = jnp.clip(jnp.exp(jax.random.uniform(own_keys[5], (NOBS,), jnp.float32, math.log(0.1), math.log(1.0))), 0.1, 1.0)
    return {"state": state, "centers": centers, "half_width": half_width, "radius": radius, "order": order, "obs_var": obs_var}


floor_level = math.exp(-2.0)

def geometry(first_row, row_count, center_rows, half_rows, radius_rows):
    rows_all = first_row + lax.iota(jnp.int32, row_count)
    distance = (rows_all[None, :] - center_rows[:, None]).astype(jnp.float32)
    half_f = half_rows.astype(jnp.float32)[:, None]
    footprint = (jnp.maximum(jnp.exp(-2.0 * distance * distance / (half_f * half_f)) - floor_level, 0.0) / jnp.sqrt(half_f)).astype(jnp.bfloat16)
    taper_rows = jnp.square(jnp.maximum(1.0 - jnp.abs(distance) / radius_rows.astype(jnp.float32)[:, None], 0.0))
    return (footprint, taper_rows)

def gain_terms(projected, variance):
    high = lax.Precision.HIGHEST
    covariance = jnp.dot(projected.T.astype(jnp.float32), projected.astype(jnp.float32), precision=high, preferred_element_type=jnp.float32) / (M - 1) + jnp.diag(variance)
    factor = jnp.linalg.cholesky(covariance)
    identity = jnp.eye(P_SIZE, dtype=jnp.float32)
    inner_inv = lax.linalg.triangular_solve(factor + jnp.diag(jnp.sqrt(variance)), identity, left_side=True, lower=True)
    gain_mat = lax.linalg.triangular_solve(factor, inner_inv, left_side=True, lower=True, transpose_a=True)
    weights = jnp.dot(projected.astype(jnp.float32), gain_mat.T.astype(jnp.float32), precision=high, preferred_element_type=jnp.float32).astype(jnp.bfloat16)
    return (weights, projected.astype(jnp.bfloat16))

def reference(state, centers, half_width, radius, order, obs_var):
    high = lax.Precision.HIGHEST
    ensemble = state
    for batch in range(BATCHES):
        picked = order[batch * P_SIZE:(batch + 1) * P_SIZE]
        footprint, taper_rows = geometry(0, NROWS, centers[picked], half_width[picked], radius[picked])
        ens_f = ensemble.astype(jnp.float32)
        projected = jnp.dot(ens_f.astype(jnp.float32), footprint.astype(jnp.float32).T.astype(jnp.float32), precision=high, preferred_element_type=jnp.float32)
        weights, projected_b = gain_terms(projected, obs_var[picked])
        cross_cov = jnp.dot(projected_b.astype(jnp.float32).T.astype(jnp.float32), ens_f.astype(jnp.float32), precision=high, preferred_element_type=jnp.float32)
        tapered = (taper_rows * cross_cov / (M - 1)).astype(jnp.bfloat16)
        ensemble = (ens_f - jnp.dot(weights.astype(jnp.float32), tapered.astype(jnp.float32), precision=high, preferred_element_type=jnp.float32)).astype(jnp.bfloat16)
    return ensemble
```

```python
import functools
import math

import jax
import jax.numpy as jnp
from jax import lax
from jax.experimental import pallas as pl
from jax.experimental.pallas import tpu as pltpu
from jax.sharding import PartitionSpec as P

M = 256
P_SIZE = 128
BATCHES = 2
BLOCK = 16
TILE = 256

FLOOR = math.exp(-2.0)
F32 = jnp.float32
BF16 = jnp.bfloat16
HIGH = lax.Precision.HIGHEST
LAST = (((1,), (1,)), ((), ()))
FIRST = (((0,), (0,)), ((), ()))


def each(start, stop, body):
    if stop - start <= 16:
        for i in range(start, stop):
            body(i)
    else:

        def step(i, carry):
            body(i)
            return carry

        lax.fori_loop(start, stop, step, 0)


def split3(x):
    high = x.astype(BF16)
    rest = x - high.astype(F32)
    mid = rest.astype(BF16)
    low = (rest - mid.astype(F32)).astype(BF16)
    return high, mid, low


def sweep(work, inv, solved, root):
    b = BLOCK
    width = work.shape[1] // P_SIZE

    def step(k, carry):
        r0 = pl.multiple_of(k * b, b)
        parts = [work[pl.ds(r0, b), g * P_SIZE : (g + 1) * P_SIZE] for g in range(width)]
        roots = root[pl.ds(r0, b), :]
        rolled = pltpu.roll(parts[0], lax.rem(P_SIZE - r0, P_SIZE), 1)
        cols = [jnp.broadcast_to(rolled[:, j : j + 1], (b, P_SIZE)) for j in range(b)]
        row_id = lax.broadcasted_iota(jnp.int32, (b, P_SIZE), 0)
        for j in range(b):
            pivot = cols[j][j : j + 1, :]
            scale = lax.rsqrt(pivot)
            scale_m = 1.0 / (pivot * scale + roots[j : j + 1, :])
            column = jnp.where(row_id > j, cols[j] * scale, 0.0)
            for i in range(j + 1, b):
                cols[i] = cols[i] - column * column[i : i + 1, :]
            for g in range(width):
                row = parts[g][j : j + 1, :] * (scale if g < 2 else scale_m)
                parts[g] = jnp.where(row_id == j, row, parts[g] - column * row)
        inv[pl.ds(r0, b), :] = parts[1]
        for g in range(2, width):
            solved[pl.ds(r0, b), (g - 2) * P_SIZE : (g - 1) * P_SIZE] = parts[g]
        pieces = [split3(x) for x in parts]
        h, m, l = pieces[0]
        left = jnp.concatenate([h, h, m, h, m, l], axis=0)
        h, m, l = (jnp.concatenate([x[n] for x in pieces], axis=1) for n in range(3))
        right = jnp.concatenate([h, m, h, l, m, h], axis=0)
        work[...] -= lax.dot_general(left, right, FIRST, preferred_element_type=F32)
        return carry

    lax.fori_loop(0, P_SIZE // b, step, 0)


def kernel(
    shape,
    state, cen, half, rad, order, var,
    out,
    e_all, foot, tap, col_c, col_r, var_b, root_b, work, inv, solved, wts,
    part, rs, ag, cpart, crs, cag,
    e_ss, e_rs, rs_ss, rs_rs, ag_ss, ag_rs,
):
    n_slab, n_mem, n_sub = shape
    n = n_slab * n_sub
    total = n * n_mem
    owners = min(n, 8)
    stride = n // owners
    chunk = P_SIZE // owners
    own, rows = state.shape
    n_tiles = rows // TILE

    mi = lax.axis_index("mem")
    me = lax.axis_index("slab") * n_sub + lax.axis_index("sub")
    mine = lax.div(me, stride)

    def peer(red, mem):
        return {"slab": lax.div(red, n_sub), "sub": lax.rem(red, n_sub), "mem": mem}

    def peer_of(off):
        red = lax.rem(me + lax.rem(off, n), n)
        mem = lax.rem(mi + lax.div(off, n), n_mem)
        return red, mem

    def owner_only(body):
        if stride == 1:
            body()
        else:
            pl.when(lax.rem(me, stride) == 0)(body)

    barrier = pltpu.get_barrier_semaphore()

    def greet(off):
        red, mem = peer_of(off)
        pl.semaphore_signal(
            barrier, inc=1, device_id=peer(red, mem), device_id_type=pl.DeviceIdType.MESH
        )

    each(1, total, greet)

    n_obs = BATCHES * P_SIZE
    picked = jnp.broadcast_to(order[...].astype(F32), (P_SIZE, n_obs)).T.astype(jnp.int32)
    lane = lax.broadcasted_iota(jnp.int32, (n_obs, P_SIZE), 1)
    masks = [picked == lane + h * P_SIZE for h in range(BATCHES)]

    def pick(ref):
        value = ref[...].astype(F32)
        chosen = 0.0
        for h in range(BATCHES):
            chosen = chosen + jnp.where(masks[h], value[:, h * P_SIZE : (h + 1) * P_SIZE], 0.0)
        return jnp.sum(chosen, axis=1, keepdims=True)

    center = pick(cen) - (me * rows).astype(F32)
    width = pick(half)
    variance = pick(var)
    col_c[...] = jnp.broadcast_to(center, (n_obs, P_SIZE))
    col_r[...] = jnp.broadcast_to(1.0 / pick(rad), (n_obs, P_SIZE))
    var_b[...] = jnp.broadcast_to(variance, (n_obs, P_SIZE))
    root_b[...] = jnp.broadcast_to(jnp.sqrt(variance), (n_obs, P_SIZE))
    steep = jnp.broadcast_to(-2.0 / (width * width), (n_obs, TILE))
    height = jnp.broadcast_to(1.0 / jnp.sqrt(width), (n_obs, TILE))
    center_w = jnp.broadcast_to(center, (n_obs, TILE))

    pl.semaphore_wait(barrier, total - 1)

    def e_copy(off):
        return pltpu.make_async_remote_copy(
            src_ref=state,
            dst_ref=e_all.at[mi],
            send_sem=e_ss.at[off],
            recv_sem=e_rs.at[mi],
            device_id=peer(me, lax.rem(mi + off, n_mem)),
            device_id_type=pl.DeviceIdType.MESH,
        )

    each(1, n_mem, lambda off: e_copy(off).start())
    e_all[mi] = state[...]

    def foot_tile(t, carry):
        at = pl.multiple_of(t * TILE, TILE)
        row = lax.broadcasted_iota(jnp.int32, (n_obs, TILE), 1) + at
        distance = row.astype(F32) - center_w
        shape_f = jnp.maximum(jnp.exp(distance * distance * steep) - FLOOR, 0.0) * height
        foot[:, pl.ds(at, TILE)] = shape_f.astype(BF16)
        return carry

    lax.fori_loop(0, n_tiles, foot_tile, 0)
    sums = lax.dot_general(foot[...], state[...], LAST, preferred_element_type=F32)
    for b in range(BATCHES):
        for o in range(owners):
            lo = b * P_SIZE + o * chunk
            part[b, o] = sums[lo : lo + chunk, :]

    def reduce_copy(source, target, x, off):
        o = lax.rem(mine + off, owners)
        return pltpu.make_async_remote_copy(
            src_ref=source.at[o],
            dst_ref=target.at[me],
            send_sem=rs_ss.at[x, off],
            recv_sem=rs_rs.at[x, me],
            device_id=peer(o * stride, mi),
            device_id_type=pl.DeviceIdType.MESH,
        )

    def reduce_start(source, target, x):
        each(1, owners, lambda off: reduce_copy(source, target, x, off).start())
        if stride > 1:
            pl.when(lax.rem(me, stride) != 0)(
                lambda: reduce_copy(source, target, x, 0).start()
            )

    def reduce_sent(source, target, x):
        each(1, owners, lambda off: reduce_copy(source, target, x, off).wait_send())
        if stride > 1:
            pl.when(lax.rem(me, stride) != 0)(
                lambda: reduce_copy(source, target, x, 0).wait_send()
            )

    def reduce_finish(source, target, x, result):
        result[...] = source[mine]

        def add(off):
            src = lax.rem(me + off, n)
            pltpu.make_async_remote_copy(
                src_ref=source.at[0],
                dst_ref=target.at[src],
                send_sem=rs_ss.at[x, 0],
                recv_sem=rs_rs.at[x, src],
                device_id=peer(src, mi),
                device_id_type=pl.DeviceIdType.MESH,
            ).wait_recv()
            result[...] += target[src]

        each(1, n, add)

    def gather_copy(block, x, off):
        red, mem = peer_of(off)
        return pltpu.make_async_remote_copy(
            src_ref=block,
            dst_ref=block,
            send_sem=ag_ss.at[x, off],
            recv_sem=ag_rs.at[x, mi * owners + mine],
            device_id=peer(red, mem),
            device_id_type=pl.DeviceIdType.MESH,
        )

    def gather_wait(ref, x, mem, o, red):
        pltpu.make_async_remote_copy(
            src_ref=ref,
            dst_ref=ref,
            send_sem=ag_ss.at[x, 0],
            recv_sem=ag_rs.at[x, mem * owners + o],
            device_id=peer(red, mem),
            device_id_type=pl.DeviceIdType.MESH,
        ).wait_recv()

    def gather_all(block_of, x, mems):
        def one(q):
            o = lax.rem(mine + lax.rem(q, owners), owners)
            mem = lax.rem(mi + lax.div(q, owners), n_mem)
            gather_wait(block_of(mem, o), x, mem, o, o * stride)

        each(1, mems * owners, one)
        if stride > 1:
            pl.when(lax.rem(me, stride) != 0)(lambda: one(0))

    for b in range(BATCHES):
        reduce_start(part.at[b], rs.at[b], b)
    for b in range(BATCHES):

        def finish(b=b):
            block = ag.at[b, mi, mine]
            reduce_finish(part.at[b], rs.at[b], b, block)
            each(1, total, lambda off: gather_copy(block, b, off).start())

        owner_only(finish)

    def slot(b, s):
        return ag[b, s].reshape(P_SIZE, own)

    def load_work(columns, b):
        cov = 0.0
        for s in range(n_mem):
            cov = cov + lax.dot_general(
                columns[s], columns[s], LAST, precision=HIGH, preferred_element_type=F32
            )
        r = lax.broadcasted_iota(jnp.int32, (P_SIZE, P_SIZE), 0)
        eye = r == lax.broadcasted_iota(jnp.int32, (P_SIZE, P_SIZE), 1)
        v = var_b[b * P_SIZE : (b + 1) * P_SIZE, :]
        work[:, :P_SIZE] = cov * (1.0 / (M - 1)) + jnp.where(eye, v, 0.0)
        work[:, P_SIZE : 2 * P_SIZE] = jnp.where(eye, 1.0, 0.0)
        for s in range(n_mem):
            lo = 2 * P_SIZE + s * own
            work[:, lo : lo + own] = columns[s]

    def taper(b, at):
        lo = b * P_SIZE
        row = lax.broadcasted_iota(jnp.int32, (P_SIZE, TILE), 1) + at
        c = jnp.concatenate([col_c[lo : lo + P_SIZE, :]] * (TILE // P_SIZE), axis=1)
        r = jnp.concatenate([col_r[lo : lo + P_SIZE, :]] * (TILE // P_SIZE), axis=1)
        near = jnp.maximum(1.0 - jnp.abs(row.astype(F32) - c) * r, 0.0)
        return near * near * (1.0 / (M - 1))

    gather_all(lambda mem, o: ag.at[0, mem, o], 0, n_mem)
    first = [slot(0, s) for s in range(n_mem)]
    load_work(first, 0)
    first_b = [x.astype(BF16) for x in first]

    def e_wait(off):
        src = lax.rem(mi + off, n_mem)
        pltpu.make_async_remote_copy(
            src_ref=state,
            dst_ref=e_all.at[src],
            send_sem=e_ss.at[0],
            recv_sem=e_rs.at[src],
            device_id=peer(me, src),
            device_id_type=pl.DeviceIdType.MESH,
        ).wait_recv()

    each(1, n_mem, e_wait)

    def cross_tile(t, carry):
        at = pl.multiple_of(t * TILE, TILE)
        cross = 0.0
        for s in range(n_mem):
            cross = cross + jnp.dot(
                first_b[s], e_all[s, :, pl.ds(at, TILE)], preferred_element_type=F32
            )
        tapered = (taper(0, at) * cross).astype(BF16)
        tap[:, pl.ds(at, TILE)] = tapered
        return carry

    lax.fori_loop(0, n_tiles, cross_tile, 0)
    change = lax.dot_general(
        foot[P_SIZE : 2 * P_SIZE, :], tap[...], LAST, preferred_element_type=F32
    )
    for o in range(owners):
        cpart[o] = change[o * chunk : (o + 1) * chunk, :]
    reduce_start(cpart, crs, BATCHES)

    sweep(work, inv, solved, root_b.at[pl.ds(0, P_SIZE)])

    def finish_change():
        block = cag.at[mine]
        reduce_finish(cpart, crs, BATCHES, block)
        each(1, n, lambda off: gather_copy(block, BATCHES, off).start())

    owner_only(finish_change)

    def weights():
        return lax.dot_general(
            solved[...], inv[...], FIRST, precision=HIGH, preferred_element_type=F32
        )

    wts[...] = weights().astype(BF16)

    gather_all(lambda mem, o: ag.at[1, mem, o], 1, n_mem)
    gather_all(lambda mem, o: cag.at[o], BATCHES, 1)
    c_full = cag[...].reshape(P_SIZE, P_SIZE)
    second = []
    for s in range(n_mem):
        moved = lax.dot_general(
            c_full,
            wts[s * own : (s + 1) * own, :].astype(F32),
            LAST,
            precision=HIGH,
            preferred_element_type=F32,
        )
        second.append(slot(1, s) - moved)
    load_work(second, 1)
    second_b = [x.astype(BF16) for x in second]

    def second_tile(t, carry):
        at = pl.multiple_of(t * TILE, TILE)
        before = tap[:, pl.ds(at, TILE)]
        cross = 0.0
        for s in range(n_mem):
            moved = jnp.dot(
                wts[s * own : (s + 1) * own, :], before, preferred_element_type=F32
            )
            now = (e_all[s, :, pl.ds(at, TILE)].astype(F32) - moved).astype(BF16)
            e_all[s, :, pl.ds(at, TILE)] = now
            cross = cross + jnp.dot(second_b[s], now, preferred_element_type=F32)
        tap[:, pl.ds(at, TILE)] = (taper(1, at) * cross).astype(BF16)
        return carry

    lax.fori_loop(0, n_tiles, second_tile, 0)
    sweep(work, inv, solved, root_b.at[pl.ds(P_SIZE, P_SIZE)])
    wts[...] = weights().astype(BF16)
    own_w = wts[pl.ds(pl.multiple_of(mi * own, own), own), :]

    def last_tile(t, carry):
        at = pl.multiple_of(t * TILE, TILE)
        moved = jnp.dot(own_w, tap[:, pl.ds(at, TILE)], preferred_element_type=F32)
        out[:, pl.ds(at, TILE)] = (
            e_all[mi, :, pl.ds(at, TILE)].astype(F32) - moved
        ).astype(BF16)
        return carry

    lax.fori_loop(0, n_tiles, last_tile, 0)

    each(1, n_mem, lambda off: e_copy(off).wait_send())
    for b in range(BATCHES):
        reduce_sent(part.at[b], rs.at[b], b)

        def sent(b=b):
            each(1, total, lambda off: gather_copy(ag.at[b, mi, mine], b, off).wait_send())

        owner_only(sent)
    reduce_sent(cpart, crs, BATCHES)

    def change_sent():
        each(1, n, lambda off: gather_copy(cag.at[mine], BATCHES, off).wait_send())

    owner_only(change_sent)


def on_device(shape, state, centers, half_width, radius, order, obs_var):
    n_slab, n_mem, n_sub = shape
    own, rows = state.shape
    n = n_slab * n_sub
    total = n * n_mem
    owners = min(n, 8)
    chunk = P_SIZE // owners
    n_obs = BATCHES * P_SIZE
    vmem = pl.BlockSpec(memory_space=pltpu.VMEM)
    return pl.pallas_call(
        functools.partial(kernel, shape),
        out_shape=jax.ShapeDtypeStruct((own, rows), BF16),
        in_specs=[vmem] * 6,
        out_specs=vmem,
        scratch_shapes=[
            pltpu.VMEM((n_mem, own, rows), BF16),
            pltpu.VMEM((n_obs, rows), BF16),
            pltpu.VMEM((P_SIZE, rows), BF16),
            pltpu.VMEM((n_obs, P_SIZE), F32),
            pltpu.VMEM((n_obs, P_SIZE), F32),
            pltpu.VMEM((n_obs, P_SIZE), F32),
            pltpu.VMEM((n_obs, P_SIZE), F32),
            pltpu.VMEM((P_SIZE, 2 * P_SIZE + M), F32),
            pltpu.VMEM((P_SIZE, P_SIZE), F32),
            pltpu.VMEM((P_SIZE, M), F32),
            pltpu.VMEM((M, P_SIZE), BF16),
            pltpu.VMEM((BATCHES, owners, chunk, own), F32),
            pltpu.VMEM((BATCHES, n, chunk, own), F32),
            pltpu.VMEM((BATCHES, n_mem, owners, chunk, own), F32),
            pltpu.VMEM((owners, chunk, P_SIZE), F32),
            pltpu.VMEM((n, chunk, P_SIZE), F32),
            pltpu.VMEM((owners, chunk, P_SIZE), F32),
            pltpu.SemaphoreType.DMA((n_mem,)),
            pltpu.SemaphoreType.DMA((n_mem,)),
            pltpu.SemaphoreType.DMA((BATCHES + 1, owners)),
            pltpu.SemaphoreType.DMA((BATCHES + 1, n)),
            pltpu.SemaphoreType.DMA((BATCHES + 1, total)),
            pltpu.SemaphoreType.DMA((BATCHES + 1, n_mem * owners)),
        ],
        compiler_params=pltpu.CompilerParams(
            collective_id=0, has_side_effects=True, vmem_limit_bytes=40 * 1024 * 1024
        ),
    )(
        state,
        centers[None, :],
        half_width[None, :],
        radius[None, :],
        order[None, :],
        obs_var[None, :],
    )


def solution(mesh):
    shape = (mesh.shape["slab"], mesh.shape["mem"], mesh.shape["sub"])
    placed = (P("mem", ("grp", "slab", "sub")), P("grp"), P("grp"), P("grp"), P("grp"), P("grp"))
    return jax.shard_map(
        functools.partial(on_device, shape),
        mesh=mesh,
        in_specs=placed,
        out_specs=P("mem", ("grp", "slab", "sub")),
        check_vma=False,
    )
```

```python
import functools
import math

import jax
import jax.numpy as jnp
from jax import lax
from jax.experimental import pallas as pl
from jax.experimental.pallas import tpu as pltpu
from jax.sharding import PartitionSpec as P

M = 256
P_SIZE = 128
BATCHES = 2
BLOCK = 16

FLOOR = math.exp(-2.0)
F32 = jnp.float32
BF16 = jnp.bfloat16
HIGH = lax.Precision.HIGHEST
LAST = (((1,), (1,)), ((), ()))
FIRST = (((0,), (0,)), ((), ()))


def each(start, stop, body):
    if stop - start <= 16:
        for i in range(start, stop):
            body(i)
    else:

        def step(i, carry):
            body(i)
            return carry

        lax.fori_loop(start, stop, step, 0)


def split3(x):
    high = x.astype(BF16)
    rest = x - high.astype(F32)
    mid = rest.astype(BF16)
    low = (rest - mid.astype(F32)).astype(BF16)
    return high, mid, low


def sweep(work, inv, solved, root):
    b = BLOCK
    width = work.shape[1] // P_SIZE

    def step(k, carry):
        r0 = pl.multiple_of(k * b, b)
        parts = [work[pl.ds(r0, b), g * P_SIZE : (g + 1) * P_SIZE] for g in range(width)]
        roots = root[pl.ds(r0, b), :]
        rolled = pltpu.roll(parts[0], lax.rem(P_SIZE - r0, P_SIZE), 1)
        cols = [jnp.broadcast_to(rolled[:, j : j + 1], (b, P_SIZE)) for j in range(b)]
        row_id = lax.broadcasted_iota(jnp.int32, (b, P_SIZE), 0)
        for j in range(b):
            pivot = cols[j][j : j + 1, :]
            scale = lax.rsqrt(pivot)
            scale_m = 1.0 / (pivot * scale + roots[j : j + 1, :])
            column = jnp.where(row_id > j, cols[j] * scale, 0.0)
            for i in range(j + 1, b):
                cols[i] = cols[i] - column * column[i : i + 1, :]
            for g in range(width):
                row = parts[g][j : j + 1, :] * (scale if g < 2 else scale_m)
                parts[g] = jnp.where(row_id == j, row, parts[g] - column * row)
        inv[pl.ds(r0, b), :] = parts[1]
        for g in range(2, width):
            solved[pl.ds(r0, b), (g - 2) * P_SIZE : (g - 1) * P_SIZE] = parts[g]
        pieces = [split3(x) for x in parts]
        h, m, l = pieces[0]
        left = jnp.concatenate([h, h, m, h, m, l], axis=0)
        h, m, l = (jnp.concatenate([x[n] for x in pieces], axis=1) for n in range(3))
        right = jnp.concatenate([h, m, h, l, m, h], axis=0)
        work[...] -= lax.dot_general(left, right, FIRST, preferred_element_type=F32)
        return carry

    lax.fori_loop(0, P_SIZE // b, step, 0)


def kernel(
    shape,
    state_hbm, cen_hbm, half_hbm, rad_hbm, order_hbm, var_hbm,
    out,
    state, cen, half, rad, order, var,
    e_all, foot, tap, tap1, col_c, col_r, var_b, root_b, work, inv, solved, wts,
    part, rs, ag, cpart, crs, cag,
    in_s, e_ss, e_rs, t_ss, t_rs, rs_ss, rs_rs, crs_ss, crs_rs, ag_ss, ag_rs, cag_ss, cag_rs,
):
    n_slab, n_mem, n_sub = shape
    n = n_slab * n_sub
    total = n * n_mem
    own, rows = state.shape
    part_rows = rows // n_mem

    mi = lax.axis_index("mem")
    me = lax.axis_index("slab") * n_sub + lax.axis_index("sub")

    def peer(red, mem):
        return {"slab": lax.div(red, n_sub), "sub": lax.rem(red, n_sub), "mem": mem}

    def peer_of(off):
        red = lax.rem(me + lax.rem(off, n), n)
        mem = lax.rem(mi + lax.div(off, n), n_mem)
        return red, mem

    inputs = [
        pltpu.make_async_copy(a, b, in_s.at[i])
        for i, (a, b) in enumerate(
            zip(
                (state_hbm, cen_hbm, half_hbm, rad_hbm, order_hbm, var_hbm),
                (state, cen, half, rad, order, var),
            )
        )
    ]
    for copy in inputs[1:] + inputs[:1]:
        copy.start()

    barrier = pltpu.get_barrier_semaphore()

    def greet(off):
        red, mem = peer_of(off)
        pl.semaphore_signal(
            barrier, inc=1, device_id=peer(red, mem), device_id_type=pl.DeviceIdType.MESH
        )

    each(1, total, greet)
    for copy in inputs[1:]:
        copy.wait()

    n_obs = BATCHES * P_SIZE
    picked = jnp.broadcast_to(order[...].astype(F32), (P_SIZE, n_obs)).T.astype(jnp.int32)
    lane = lax.broadcasted_iota(jnp.int32, (n_obs, P_SIZE), 1)
    masks = [picked == lane + h * P_SIZE for h in range(BATCHES)]

    def pick(ref):
        value = ref[...].astype(F32)
        chosen = 0.0
        for h in range(BATCHES):
            chosen = chosen + jnp.where(masks[h], value[:, h * P_SIZE : (h + 1) * P_SIZE], 0.0)
        return jnp.sum(chosen, axis=1, keepdims=True)

    center = pick(cen) - (me * rows).astype(F32)
    width = pick(half)
    variance = pick(var)
    col_c[...] = jnp.broadcast_to(center, (n_obs, P_SIZE))
    col_r[...] = jnp.broadcast_to(1.0 / pick(rad), (n_obs, P_SIZE))
    var_b[...] = jnp.broadcast_to(variance, (n_obs, P_SIZE))
    root_b[...] = jnp.broadcast_to(jnp.sqrt(variance), (n_obs, P_SIZE))
    steep = -2.0 / (width * width)
    height = 1.0 / jnp.sqrt(width)

    pl.semaphore_wait(barrier, total - 1)

    def rows_of(mem):
        return pl.ds(pl.multiple_of(mem * part_rows, part_rows), part_rows)

    my_rows = rows_of(mi)

    def e_copy(off):
        to = lax.rem(mi + off, n_mem)
        return pltpu.make_async_remote_copy(
            src_ref=state_hbm.at[:, rows_of(to)],
            dst_ref=e_all.at[mi],
            send_sem=e_ss.at[off],
            recv_sem=e_rs.at[mi],
            device_id=peer(me, to),
            device_id_type=pl.DeviceIdType.MESH,
        )

    each(1, n_mem, lambda off: e_copy(off).start())

    def foot_tile(t, carry):
        at = pl.multiple_of(t * 256, 256)
        row = lax.broadcasted_iota(jnp.int32, (n_obs, 256), 1) + at
        distance = row.astype(F32) - center
        shape_f = jnp.maximum(jnp.exp(distance * distance * steep) - FLOOR, 0.0) * height
        foot[:, pl.ds(at, 256)] = shape_f.astype(BF16)
        return carry

    lax.fori_loop(0, rows // 256, foot_tile, 0)
    inputs[0].wait()
    e_all[mi] = state[:, my_rows]
    sums = lax.dot_general(foot[...], state[...], LAST, preferred_element_type=F32)
    for b in range(BATCHES):
        part[b] = sums[b * P_SIZE : (b + 1) * P_SIZE, :].reshape(part.shape[1:])

    class Sum:
        def __init__(self, size, index, device, source, target, result, everyone, sems):
            self.size, self.index, self.device = size, index, device
            self.source, self.target, self.result, self.everyone = source, target, result, everyone
            self.rs_ss, self.rs_rs, self.ag_ss, self.ag_rs = sems
            self.owners = source.shape[0]
            self.stride = size // self.owners
            self.mine = lax.div(index, self.stride)

        def remote(self, src, dst, send, recv, device):
            return pltpu.make_async_remote_copy(
                src_ref=src, dst_ref=dst, send_sem=send, recv_sem=recv,
                device_id=device, device_id_type=pl.DeviceIdType.MESH,
            )

        def if_owner(self, body, owner=True):
            if self.stride == 1:
                if owner:
                    body()
            else:
                pl.when((lax.rem(self.index, self.stride) == 0) == owner)(body)

        def out_copy(self, off):
            o = lax.rem(self.mine + off, self.owners)
            return self.remote(
                self.source.at[o], self.target.at[self.index],
                self.rs_ss.at[off], self.rs_rs.at[self.index], self.device(o * self.stride),
            )

        def start(self):
            each(1, self.owners, lambda off: self.out_copy(off).start())
            self.if_owner(lambda: self.out_copy(0).start(), False)

        def gather_copy(self, off):
            block = self.result(mi, self.mine)
            return self.remote(
                block, block, self.ag_ss.at[off],
                self.ag_rs.at[mi if self.everyone else 0, self.mine], peer(*peer_of(off)),
            )

        def finish(self):
            def body():
                for off in range(1, self.size) if self.size <= 16 else ():
                    self.arrived(lax.rem(self.index + off, self.size))
                block = self.result(mi, self.mine)
                value = self.source[self.mine]
                if self.size <= 16:
                    for off in range(1, self.size):
                        value = value + self.target[lax.rem(self.index + off, self.size)]
                    block[...] = value
                else:
                    block[...] = value

                    def add(off):
                        src = lax.rem(self.index + off, self.size)
                        self.arrived(src)
                        block[...] += self.target[src]

                    each(1, self.size, add)
                each(1, total, lambda off: self.gather_copy(off).start())

            self.if_owner(body)

        def arrived(self, src):
            self.remote(
                self.source.at[0], self.target.at[src], self.rs_ss.at[0], self.rs_rs.at[src],
                self.device(src),
            ).wait_recv()

        def gather(self):
            mems = n_mem if self.everyone else 1

            def one(q):
                o = lax.rem(self.mine + lax.rem(q, self.owners), self.owners)
                mem = lax.rem(mi + lax.div(q, self.owners), n_mem)
                block = self.result(mem, o)
                self.remote(
                    block, block, self.ag_ss.at[0],
                    self.ag_rs.at[mem if self.everyone else 0, o],
                    self.device(o * self.stride),
                ).wait_recv()

            each(1, mems * self.owners, one)
            self.if_owner(lambda: one(0), False)

        def sent(self):
            each(1, self.owners, lambda off: self.out_copy(off).wait_send())
            self.if_owner(lambda: self.out_copy(0).wait_send(), False)
            self.if_owner(
                lambda: each(1, total, lambda off: self.gather_copy(off).wait_send())
            )

    projections = [
        Sum(
            n, me, lambda i: peer(i, mi), part.at[b], rs.at[b],
            lambda mem, o, b=b: ag.at[b, mem, o], True,
            (rs_ss.at[b], rs_rs.at[b], ag_ss.at[b], ag_rs.at[b]),
        )
        for b in range(BATCHES)
    ]
    changes = Sum(
        total, mi * n + me, lambda i: peer(lax.rem(i, n), lax.div(i, n)), cpart, crs,
        lambda mem, o: cag.at[o], False, (crs_ss, crs_rs, cag_ss, cag_rs),
    )
    for x in projections:
        x.start()
    for x in projections:
        x.finish()

    def slot(b, s):
        return ag[b, s].reshape(P_SIZE, own)

    def load_work(columns, b):
        cov = 0.0
        for s in range(n_mem):
            cov = cov + lax.dot_general(
                columns[s], columns[s], LAST, precision=HIGH, preferred_element_type=F32
            )
        r = lax.broadcasted_iota(jnp.int32, (P_SIZE, P_SIZE), 0)
        eye = r == lax.broadcasted_iota(jnp.int32, (P_SIZE, P_SIZE), 1)
        v = var_b[b * P_SIZE : (b + 1) * P_SIZE, :]
        work[:, :P_SIZE] = cov * (1.0 / (M - 1)) + jnp.where(eye, v, 0.0)
        work[:, P_SIZE : 2 * P_SIZE] = jnp.where(eye, 1.0, 0.0)
        for s in range(n_mem):
            lo = 2 * P_SIZE + s * own
            work[:, lo : lo + own] = columns[s]

    def taper(b):
        lo = b * P_SIZE
        row = lax.broadcasted_iota(jnp.int32, (P_SIZE, part_rows), 1) + mi * part_rows
        c = jnp.concatenate([col_c[lo : lo + P_SIZE, :]] * (part_rows // P_SIZE), axis=1)
        r = jnp.concatenate([col_r[lo : lo + P_SIZE, :]] * (part_rows // P_SIZE), axis=1)
        near = jnp.maximum(1.0 - jnp.abs(row.astype(F32) - c) * r, 0.0)
        return near * near * (1.0 / (M - 1))

    def t_copy(x, ref, off):
        return pltpu.make_async_remote_copy(
            src_ref=ref.at[mi],
            dst_ref=ref.at[mi],
            send_sem=t_ss.at[x, off],
            recv_sem=t_rs.at[x, mi],
            device_id=peer(me, lax.rem(mi + off, n_mem)),
            device_id_type=pl.DeviceIdType.MESH,
        )

    def t_wait(x, ref, off):
        src = lax.rem(mi + off, n_mem)
        pltpu.make_async_remote_copy(
            src_ref=ref.at[src],
            dst_ref=ref.at[src],
            send_sem=t_ss.at[x, 0],
            recv_sem=t_rs.at[x, src],
            device_id=peer(me, src),
            device_id_type=pl.DeviceIdType.MESH,
        ).wait_recv()

    projections[0].gather()
    first = [slot(0, s) for s in range(n_mem)]
    first_b = [x.astype(BF16) for x in first]

    def e_wait(off):
        src = lax.rem(mi + off, n_mem)
        pltpu.make_async_remote_copy(
            src_ref=e_all.at[src],
            dst_ref=e_all.at[src],
            send_sem=e_ss.at[0],
            recv_sem=e_rs.at[src],
            device_id=peer(me, src),
            device_id_type=pl.DeviceIdType.MESH,
        ).wait_recv()

    each(1, n_mem, e_wait)

    cross = 0.0
    for s in range(n_mem):
        cross = cross + jnp.dot(first_b[s], e_all[s], preferred_element_type=F32)
    before = (taper(0) * cross).astype(BF16)
    tap[mi] = before
    change = lax.dot_general(
        foot[P_SIZE : 2 * P_SIZE, my_rows], before, LAST, preferred_element_type=F32
    )
    cpart[...] = change.reshape(cpart.shape)
    changes.start()
    each(1, n_mem, lambda off: t_copy(0, tap, off).start())

    load_work(first, 0)
    sweep(work, inv, solved, root_b.at[pl.ds(0, P_SIZE)])
    changes.finish()

    def weights():
        return lax.dot_general(
            solved[...], inv[...], FIRST, precision=HIGH, preferred_element_type=F32
        )

    wts[...] = weights().astype(BF16)

    projections[1].gather()
    changes.gather()
    c_full = cag[...].reshape(P_SIZE, P_SIZE)
    second = []
    for s in range(n_mem):
        moved = lax.dot_general(
            c_full,
            wts[s * own : (s + 1) * own, :].astype(F32),
            LAST,
            precision=HIGH,
            preferred_element_type=F32,
        )
        second.append(slot(1, s) - moved)
    second_b = [x.astype(BF16) for x in second]

    before = tap[mi]
    cross = 0.0
    for s in range(n_mem):
        moved = jnp.dot(wts[s * own : (s + 1) * own, :], before, preferred_element_type=F32)
        now = (e_all[s].astype(F32) - moved).astype(BF16)
        cross = cross + jnp.dot(second_b[s], now, preferred_element_type=F32)
    tap1[mi] = (taper(1) * cross).astype(BF16)
    each(1, n_mem, lambda off: t_copy(1, tap1, off).start())

    load_work(second, 1)
    own_w = wts[pl.ds(pl.multiple_of(mi * own, own), own), :]
    each(1, n_mem, lambda off: t_wait(0, tap, off))
    for mem in range(n_mem):
        at = slice(mem * part_rows, (mem + 1) * part_rows)
        moved = jnp.dot(own_w, tap[mem], preferred_element_type=F32)
        out[:, at] = (state[:, at].astype(F32) - moved).astype(BF16)

    sweep(work, inv, solved, root_b.at[pl.ds(P_SIZE, P_SIZE)])
    wts[...] = weights().astype(BF16)
    own_w = wts[pl.ds(pl.multiple_of(mi * own, own), own), :]

    each(1, n_mem, lambda off: t_wait(1, tap1, off))
    for mem in range(n_mem):
        at = slice(mem * part_rows, (mem + 1) * part_rows)
        moved = jnp.dot(own_w, tap1[mem], preferred_element_type=F32)
        out[:, at] = (out[:, at].astype(F32) - moved).astype(BF16)

    each(1, n_mem, lambda off: e_copy(off).wait_send())
    for x, ref in enumerate((tap, tap1)):
        each(1, n_mem, lambda off: t_copy(x, ref, off).wait_send())
    for x in projections + [changes]:
        x.sent()


def on_device(shape, state, centers, half_width, radius, order, obs_var):
    n_slab, n_mem, n_sub = shape
    own, rows = state.shape
    n = n_slab * n_sub
    total = n * n_mem
    owners = min(n, 8)
    chunk = P_SIZE // owners
    c_owners = min(total, 16)
    c_chunk = P_SIZE // c_owners
    n_obs = BATCHES * P_SIZE
    part_rows = rows // n_mem
    hbm = pl.BlockSpec(memory_space=pltpu.HBM)
    vmem = pl.BlockSpec(memory_space=pltpu.VMEM)
    return pl.pallas_call(
        functools.partial(kernel, shape),
        out_shape=jax.ShapeDtypeStruct((own, rows), BF16),
        in_specs=[hbm] * 6,
        out_specs=vmem,
        scratch_shapes=[
            pltpu.VMEM((own, rows), BF16),
            pltpu.VMEM((1, n_obs), jnp.int32),
            pltpu.VMEM((1, n_obs), jnp.int32),
            pltpu.VMEM((1, n_obs), jnp.int32),
            pltpu.VMEM((1, n_obs), jnp.int32),
            pltpu.VMEM((1, n_obs), F32),
            pltpu.VMEM((n_mem, own, part_rows), BF16),
            pltpu.VMEM((n_obs, rows), BF16),
            pltpu.VMEM((n_mem, P_SIZE, part_rows), BF16),
            pltpu.VMEM((n_mem, P_SIZE, part_rows), BF16),
            pltpu.VMEM((n_obs, P_SIZE), F32),
            pltpu.VMEM((n_obs, P_SIZE), F32),
            pltpu.VMEM((n_obs, P_SIZE), F32),
            pltpu.VMEM((n_obs, P_SIZE), F32),
            pltpu.VMEM((P_SIZE, 2 * P_SIZE + M), F32),
            pltpu.VMEM((P_SIZE, P_SIZE), F32),
            pltpu.VMEM((P_SIZE, M), F32),
            pltpu.VMEM((M, P_SIZE), BF16),
            pltpu.VMEM((BATCHES, owners, chunk, own), F32),
            pltpu.VMEM((BATCHES, n, chunk, own), F32),
            pltpu.VMEM((BATCHES, n_mem, owners, chunk, own), F32),
            pltpu.VMEM((c_owners, c_chunk, P_SIZE), F32),
            pltpu.VMEM((total, c_chunk, P_SIZE), F32),
            pltpu.VMEM((c_owners, c_chunk, P_SIZE), F32),
            pltpu.SemaphoreType.DMA((6,)),
            pltpu.SemaphoreType.DMA((n_mem,)),
            pltpu.SemaphoreType.DMA((n_mem,)),
            pltpu.SemaphoreType.DMA((BATCHES, n_mem)),
            pltpu.SemaphoreType.DMA((BATCHES, n_mem)),
            pltpu.SemaphoreType.DMA((BATCHES, owners)),
            pltpu.SemaphoreType.DMA((BATCHES, n)),
            pltpu.SemaphoreType.DMA((c_owners,)),
            pltpu.SemaphoreType.DMA((total,)),
            pltpu.SemaphoreType.DMA((BATCHES, total)),
            pltpu.SemaphoreType.DMA((BATCHES, n_mem, owners)),
            pltpu.SemaphoreType.DMA((total,)),
            pltpu.SemaphoreType.DMA((1, c_owners)),
        ],
        compiler_params=pltpu.CompilerParams(
            collective_id=0, has_side_effects=True, vmem_limit_bytes=40 * 1024 * 1024
        ),
    )(
        state,
        centers[None, :],
        half_width[None, :],
        radius[None, :],
        order[None, :],
        obs_var[None, :],
    )


def solution(mesh):
    shape = (mesh.shape["slab"], mesh.shape["mem"], mesh.shape["sub"])
    placed = (P("mem", ("grp", "slab", "sub")), P("grp"), P("grp"), P("grp"), P("grp"), P("grp"))
    return jax.shard_map(
        functools.partial(on_device, shape),
        mesh=mesh,
        in_specs=placed,
        out_specs=P("mem", ("grp", "slab", "sub")),
        check_vma=False,
    )
```

```python
import functools
import math

import jax
import jax.numpy as jnp
from jax import lax
from jax.experimental import pallas as pl
from jax.experimental.pallas import tpu as pltpu
from jax.sharding import PartitionSpec as P

M = 256
P_SIZE = 128
BATCHES = 2
BLOCK = 16
SPLIT = 4
SPLIT_2 = 4

FLOOR = math.exp(-2.0)
F32 = jnp.float32
BF16 = jnp.bfloat16
HIGH = lax.Precision.HIGHEST
LAST = (((1,), (1,)), ((), ()))
FIRST = (((0,), (0,)), ((), ()))


def each(start, stop, body):
    if stop - start <= 16:
        for i in range(start, stop):
            body(i)
    else:

        def step(i, carry):
            body(i)
            return carry

        lax.fori_loop(start, stop, step, 0)


def split3(x):
    high = x.astype(BF16)
    rest = x - high.astype(F32)
    mid = rest.astype(BF16)
    low = (rest - mid.astype(F32)).astype(BF16)
    return high, mid, low


def sweep(work, inv, solved, root, first=0, last=P_SIZE // BLOCK):
    b = BLOCK
    width = work.shape[1] // P_SIZE

    def step(k, carry):
        r0 = pl.multiple_of(k * b, b)
        parts = [work[pl.ds(r0, b), g * P_SIZE : (g + 1) * P_SIZE] for g in range(width)]
        roots = root[pl.ds(r0, b), :]
        rolled = pltpu.roll(parts[0], lax.rem(P_SIZE - r0, P_SIZE), 1)
        cols = [jnp.broadcast_to(rolled[:, j : j + 1], (b, P_SIZE)) for j in range(b)]
        row_id = lax.broadcasted_iota(jnp.int32, (b, P_SIZE), 0)
        for j in range(b):
            pivot = cols[j][j : j + 1, :]
            scale = lax.rsqrt(pivot)
            scale_m = 1.0 / (pivot * scale + roots[j : j + 1, :])
            column = jnp.where(row_id > j, cols[j] * scale, 0.0)
            for i in range(j + 1, b):
                cols[i] = cols[i] - column * column[i : i + 1, :]
            for g in range(width):
                row = parts[g][j : j + 1, :] * (scale if g < 2 else scale_m)
                parts[g] = jnp.where(row_id == j, row, parts[g] - column * row)
        inv[pl.ds(r0, b), :] = parts[1]
        for g in range(2, width):
            solved[pl.ds(r0, b), (g - 2) * P_SIZE : (g - 1) * P_SIZE] = parts[g]
        pieces = [split3(x) for x in parts]
        h, m, l = pieces[0]
        left = jnp.concatenate([h, h, m, h, m, l], axis=0)
        h, m, l = (jnp.concatenate([x[n] for x in pieces], axis=1) for n in range(3))
        right = jnp.concatenate([h, m, h, l, m, h], axis=0)
        work[...] -= lax.dot_general(left, right, FIRST, preferred_element_type=F32)
        return carry

    lax.fori_loop(first, last, step, 0)


def kernel(
    shape,
    state_hbm, cen_hbm, half_hbm, rad_hbm, order_hbm, var_hbm,
    out,
    state, cen, half, rad, order, var,
    e_all, foot, tap, tap1, col_c, col_r, var_b, root_b, work, inv, solved, wts,
    part, rs, ag, cpart, crs, cag,
    in_s, e_ss, e_rs, t_ss, t_rs, rs_ss, rs_rs, crs_ss, crs_rs, ag_ss, ag_rs, cag_ss, cag_rs,
):
    n_slab, n_mem, n_sub = shape
    n = n_slab * n_sub
    total = n * n_mem
    own, rows = state.shape
    part_rows = rows // n_mem

    mi = lax.axis_index("mem")
    me = lax.axis_index("slab") * n_sub + lax.axis_index("sub")

    def peer(red, mem):
        return {"slab": lax.div(red, n_sub), "sub": lax.rem(red, n_sub), "mem": mem}

    def peer_of(off):
        red = lax.rem(me + lax.rem(off, n), n)
        mem = lax.rem(mi + lax.div(off, n), n_mem)
        return red, mem

    inputs = [
        pltpu.make_async_copy(a, b, in_s.at[i])
        for i, (a, b) in enumerate(
            zip(
                (state_hbm, cen_hbm, half_hbm, rad_hbm, order_hbm, var_hbm),
                (state, cen, half, rad, order, var),
            )
        )
    ]
    for copy in inputs[1:] + inputs[:1]:
        copy.start()

    barrier = pltpu.get_barrier_semaphore()

    def greet(off):
        red, mem = peer_of(off)
        pl.semaphore_signal(
            barrier, inc=1, device_id=peer(red, mem), device_id_type=pl.DeviceIdType.MESH
        )

    each(1, total, greet)
    for copy in inputs[1:]:
        copy.wait()

    n_obs = BATCHES * P_SIZE
    picked = jnp.broadcast_to(order[...].astype(F32), (P_SIZE, n_obs)).T.astype(jnp.int32)
    lane = lax.broadcasted_iota(jnp.int32, (n_obs, P_SIZE), 1)
    masks = [picked == lane + h * P_SIZE for h in range(BATCHES)]

    def pick(ref):
        value = ref[...].astype(F32)
        chosen = 0.0
        for h in range(BATCHES):
            chosen = chosen + jnp.where(masks[h], value[:, h * P_SIZE : (h + 1) * P_SIZE], 0.0)
        return jnp.sum(chosen, axis=1, keepdims=True)

    center = pick(cen) - (me * rows).astype(F32)
    width = pick(half)
    variance = pick(var)
    col_c[...] = jnp.broadcast_to(center, (n_obs, P_SIZE))
    col_r[...] = jnp.broadcast_to(1.0 / pick(rad), (n_obs, P_SIZE))
    var_b[...] = jnp.broadcast_to(variance, (n_obs, P_SIZE))
    root_b[...] = jnp.broadcast_to(jnp.sqrt(variance), (n_obs, P_SIZE))
    steep = -2.0 / (width * width)
    height = 1.0 / jnp.sqrt(width)

    def rows_of(mem):
        return pl.ds(pl.multiple_of(mem * part_rows, part_rows), part_rows)

    my_rows = rows_of(mi)

    def e_copy(off):
        to = lax.rem(mi + off, n_mem)
        return pltpu.make_async_remote_copy(
            src_ref=state_hbm.at[:, rows_of(to)],
            dst_ref=e_all.at[mi],
            send_sem=e_ss.at[off],
            recv_sem=e_rs.at[mi],
            device_id=peer(me, to),
            device_id_type=pl.DeviceIdType.MESH,
        )

    def foot_tile(t, carry):
        at = pl.multiple_of(t * 256, 256)
        row = lax.broadcasted_iota(jnp.int32, (n_obs, 256), 1) + at
        distance = row.astype(F32) - center
        shape_f = jnp.maximum(jnp.exp(distance * distance * steep) - FLOOR, 0.0) * height
        foot[:, pl.ds(at, 256)] = shape_f.astype(BF16)
        return carry

    lax.fori_loop(0, rows // 256, foot_tile, 0)
    inputs[0].wait()
    sums = lax.dot_general(foot[...], state[...], LAST, preferred_element_type=F32)
    for b in range(BATCHES):
        part[b] = sums[b * P_SIZE : (b + 1) * P_SIZE, :].reshape(part.shape[1:])

    class Sum:
        def __init__(self, size, index, device, source, target, result, everyone, sems):
            self.size, self.index, self.device = size, index, device
            self.source, self.target, self.result, self.everyone = source, target, result, everyone
            self.rs_ss, self.rs_rs, self.ag_ss, self.ag_rs = sems
            self.owners = source.shape[0]
            self.stride = size // self.owners
            self.mine = lax.div(index, self.stride)

        def remote(self, src, dst, send, recv, device):
            return pltpu.make_async_remote_copy(
                src_ref=src, dst_ref=dst, send_sem=send, recv_sem=recv,
                device_id=device, device_id_type=pl.DeviceIdType.MESH,
            )

        def if_owner(self, body, owner=True):
            if self.stride == 1:
                if owner:
                    body()
            else:
                pl.when((lax.rem(self.index, self.stride) == 0) == owner)(body)

        def out_copy(self, off):
            o = lax.rem(self.mine + off, self.owners)
            return self.remote(
                self.source.at[o], self.target.at[self.index],
                self.rs_ss.at[off], self.rs_rs.at[self.index], self.device(o * self.stride),
            )

        def start(self):
            each(1, self.owners, lambda off: self.out_copy(off).start())
            self.if_owner(lambda: self.out_copy(0).start(), False)

        def gather_copy(self, off):
            block = self.result(mi, self.mine)
            return self.remote(
                block, block, self.ag_ss.at[off],
                self.ag_rs.at[mi if self.everyone else 0, self.mine], peer(*peer_of(off)),
            )

        def finish(self):
            def body():
                for off in range(1, self.size) if self.size <= 16 else ():
                    self.arrived(lax.rem(self.index + off, self.size))
                block = self.result(mi, self.mine)
                value = self.source[self.mine]
                if self.size <= 16:
                    for off in range(1, self.size):
                        value = value + self.target[lax.rem(self.index + off, self.size)]
                    block[...] = value
                else:
                    block[...] = value

                    def add(off):
                        src = lax.rem(self.index + off, self.size)
                        self.arrived(src)
                        block[...] += self.target[src]

                    each(1, self.size, add)
                each(1, total, lambda off: self.gather_copy(off).start())

            self.if_owner(body)

        def arrived(self, src):
            self.remote(
                self.source.at[0], self.target.at[src], self.rs_ss.at[0], self.rs_rs.at[src],
                self.device(src),
            ).wait_recv()

        def gather(self):
            mems = n_mem if self.everyone else 1

            def one(q):
                o = lax.rem(self.mine + lax.rem(q, self.owners), self.owners)
                mem = lax.rem(mi + lax.div(q, self.owners), n_mem)
                block = self.result(mem, o)
                self.remote(
                    block, block, self.ag_ss.at[0],
                    self.ag_rs.at[mem if self.everyone else 0, o],
                    self.device(o * self.stride),
                ).wait_recv()

            each(1, mems * self.owners, one)
            self.if_owner(lambda: one(0), False)

        def sent(self):
            each(1, self.owners, lambda off: self.out_copy(off).wait_send())
            self.if_owner(lambda: self.out_copy(0).wait_send(), False)
            self.if_owner(
                lambda: each(1, total, lambda off: self.gather_copy(off).wait_send())
            )

    projections = [
        Sum(
            n, me, lambda i: peer(i, mi), part.at[b], rs.at[b],
            lambda mem, o, b=b: ag.at[b, mem, o], True,
            (rs_ss.at[b], rs_rs.at[b], ag_ss.at[b], ag_rs.at[b]),
        )
        for b in range(BATCHES)
    ]
    changes = Sum(
        total, mi * n + me, lambda i: peer(lax.rem(i, n), lax.div(i, n)), cpart, crs,
        lambda mem, o: cag.at[o], False, (crs_ss, crs_rs, cag_ss, cag_rs),
    )
    pl.semaphore_wait(barrier, total - 1)
    for x in projections:
        x.start()
    each(1, n_mem, lambda off: e_copy(off).start())
    e_all[mi] = state[:, my_rows]
    projections[0].finish()

    def slot(b, s):
        return ag[b, s].reshape(P_SIZE, own)

    def load_work(columns, b):
        cov = 0.0
        for s in range(n_mem):
            cov = cov + lax.dot_general(
                columns[s], columns[s], LAST, precision=HIGH, preferred_element_type=F32
            )
        r = lax.broadcasted_iota(jnp.int32, (P_SIZE, P_SIZE), 0)
        eye = r == lax.broadcasted_iota(jnp.int32, (P_SIZE, P_SIZE), 1)
        v = var_b[b * P_SIZE : (b + 1) * P_SIZE, :]
        work[:, :P_SIZE] = cov * (1.0 / (M - 1)) + jnp.where(eye, v, 0.0)
        work[:, P_SIZE : 2 * P_SIZE] = jnp.where(eye, 1.0, 0.0)
        for s in range(n_mem):
            lo = 2 * P_SIZE + s * own
            work[:, lo : lo + own] = columns[s]

    def taper(b):
        lo = b * P_SIZE
        row = lax.broadcasted_iota(jnp.int32, (P_SIZE, part_rows), 1) + mi * part_rows
        c = jnp.concatenate([col_c[lo : lo + P_SIZE, :]] * (part_rows // P_SIZE), axis=1)
        r = jnp.concatenate([col_r[lo : lo + P_SIZE, :]] * (part_rows // P_SIZE), axis=1)
        near = jnp.maximum(1.0 - jnp.abs(row.astype(F32) - c) * r, 0.0)
        return near * near * (1.0 / (M - 1))

    def t_copy(x, ref, off):
        return pltpu.make_async_remote_copy(
            src_ref=ref.at[mi],
            dst_ref=ref.at[mi],
            send_sem=t_ss.at[x, off],
            recv_sem=t_rs.at[x, mi],
            device_id=peer(me, lax.rem(mi + off, n_mem)),
            device_id_type=pl.DeviceIdType.MESH,
        )

    def t_wait(x, ref, off):
        src = lax.rem(mi + off, n_mem)
        pltpu.make_async_remote_copy(
            src_ref=ref.at[src],
            dst_ref=ref.at[src],
            send_sem=t_ss.at[x, 0],
            recv_sem=t_rs.at[x, src],
            device_id=peer(me, src),
            device_id_type=pl.DeviceIdType.MESH,
        ).wait_recv()

    projections[0].gather()
    first = [slot(0, s) for s in range(n_mem)]
    first_b = [x.astype(BF16) for x in first]

    def e_wait(off):
        src = lax.rem(mi + off, n_mem)
        pltpu.make_async_remote_copy(
            src_ref=e_all.at[src],
            dst_ref=e_all.at[src],
            send_sem=e_ss.at[0],
            recv_sem=e_rs.at[src],
            device_id=peer(me, src),
            device_id_type=pl.DeviceIdType.MESH,
        ).wait_recv()

    each(1, n_mem, e_wait)

    cross = 0.0
    for s in range(n_mem):
        cross = cross + jnp.dot(first_b[s], e_all[s], preferred_element_type=F32)
    before = (taper(0) * cross).astype(BF16)
    tap[mi] = before
    change = lax.dot_general(
        foot[P_SIZE : 2 * P_SIZE, my_rows], before, LAST, preferred_element_type=F32
    )
    cpart[...] = change.reshape(cpart.shape)
    changes.start()
    projections[1].finish()

    load_work(first, 0)
    sweep(work, inv, solved, root_b.at[pl.ds(0, P_SIZE)], 0, SPLIT)
    changes.finish()
    each(1, n_mem, lambda off: t_copy(0, tap, off).start())
    sweep(work, inv, solved, root_b.at[pl.ds(0, P_SIZE)], SPLIT)

    def weights():
        return lax.dot_general(
            solved[...], inv[...], FIRST, precision=HIGH, preferred_element_type=F32
        )

    wts[...] = weights().astype(BF16)

    projections[1].gather()
    changes.gather()
    c_full = cag[...].reshape(P_SIZE, P_SIZE)
    second = []
    for s in range(n_mem):
        moved = lax.dot_general(
            c_full,
            wts[s * own : (s + 1) * own, :].astype(F32),
            LAST,
            precision=HIGH,
            preferred_element_type=F32,
        )
        second.append(slot(1, s) - moved)
    second_b = [x.astype(BF16) for x in second]

    before = tap[mi]
    cross = 0.0
    for s in range(n_mem):
        moved = jnp.dot(wts[s * own : (s + 1) * own, :], before, preferred_element_type=F32)
        now = (e_all[s].astype(F32) - moved).astype(BF16)
        cross = cross + jnp.dot(second_b[s], now, preferred_element_type=F32)
    tap1[mi] = (taper(1) * cross).astype(BF16)
    each(1, n_mem, lambda off: t_copy(1, tap1, off).start())

    load_work(second, 1)
    own_w = wts[pl.ds(pl.multiple_of(mi * own, own), own), :]
    sweep(work, inv, solved, root_b.at[pl.ds(P_SIZE, P_SIZE)], 0, SPLIT_2)
    each(1, n_mem, lambda off: t_wait(0, tap, off))
    for mem in range(n_mem):
        at = slice(mem * part_rows, (mem + 1) * part_rows)
        moved = jnp.dot(own_w, tap[mem], preferred_element_type=F32)
        out[:, at] = (state[:, at].astype(F32) - moved).astype(BF16)
    sweep(work, inv, solved, root_b.at[pl.ds(P_SIZE, P_SIZE)], SPLIT_2)
    wts[...] = weights().astype(BF16)
    own_w = wts[pl.ds(pl.multiple_of(mi * own, own), own), :]

    each(1, n_mem, lambda off: t_wait(1, tap1, off))
    for mem in range(n_mem):
        at = slice(mem * part_rows, (mem + 1) * part_rows)
        moved = jnp.dot(own_w, tap1[mem], preferred_element_type=F32)
        out[:, at] = (out[:, at].astype(F32) - moved).astype(BF16)

    each(1, n_mem, lambda off: e_copy(off).wait_send())
    for x, ref in enumerate((tap, tap1)):
        each(1, n_mem, lambda off: t_copy(x, ref, off).wait_send())
    for x in projections + [changes]:
        x.sent()


def on_device(shape, state, centers, half_width, radius, order, obs_var):
    n_slab, n_mem, n_sub = shape
    own, rows = state.shape
    n = n_slab * n_sub
    total = n * n_mem
    owners = min(n, 4)
    chunk = P_SIZE // owners
    c_owners = min(total, 8)
    c_chunk = P_SIZE // c_owners
    n_obs = BATCHES * P_SIZE
    part_rows = rows // n_mem
    hbm = pl.BlockSpec(memory_space=pltpu.HBM)
    vmem = pl.BlockSpec(memory_space=pltpu.VMEM)
    return pl.pallas_call(
        functools.partial(kernel, shape),
        out_shape=jax.ShapeDtypeStruct((own, rows), BF16),
        in_specs=[hbm] * 6,
        out_specs=vmem,
        scratch_shapes=[
            pltpu.VMEM((own, rows), BF16),
            pltpu.VMEM((1, n_obs), jnp.int32),
            pltpu.VMEM((1, n_obs), jnp.int32),
            pltpu.VMEM((1, n_obs), jnp.int32),
            pltpu.VMEM((1, n_obs), jnp.int32),
            pltpu.VMEM((1, n_obs), F32),
            pltpu.VMEM((n_mem, own, part_rows), BF16),
            pltpu.VMEM((n_obs, rows), BF16),
            pltpu.VMEM((n_mem, P_SIZE, part_rows), BF16),
            pltpu.VMEM((n_mem, P_SIZE, part_rows), BF16),
            pltpu.VMEM((n_obs, P_SIZE), F32),
            pltpu.VMEM((n_obs, P_SIZE), F32),
            pltpu.VMEM((n_obs, P_SIZE), F32),
            pltpu.VMEM((n_obs, P_SIZE), F32),
            pltpu.VMEM((P_SIZE, 2 * P_SIZE + M), F32),
            pltpu.VMEM((P_SIZE, P_SIZE), F32),
            pltpu.VMEM((P_SIZE, M), F32),
            pltpu.VMEM((M, P_SIZE), BF16),
            pltpu.VMEM((BATCHES, owners, chunk, own), F32),
            pltpu.VMEM((BATCHES, n, chunk, own), F32),
            pltpu.VMEM((BATCHES, n_mem, owners, chunk, own), F32),
            pltpu.VMEM((c_owners, c_chunk, P_SIZE), F32),
            pltpu.VMEM((total, c_chunk, P_SIZE), F32),
            pltpu.VMEM((c_owners, c_chunk, P_SIZE), F32),
            pltpu.SemaphoreType.DMA((6,)),
            pltpu.SemaphoreType.DMA((n_mem,)),
            pltpu.SemaphoreType.DMA((n_mem,)),
            pltpu.SemaphoreType.DMA((BATCHES, n_mem)),
            pltpu.SemaphoreType.DMA((BATCHES, n_mem)),
            pltpu.SemaphoreType.DMA((BATCHES, owners)),
            pltpu.SemaphoreType.DMA((BATCHES, n)),
            pltpu.SemaphoreType.DMA((c_owners,)),
            pltpu.SemaphoreType.DMA((total,)),
            pltpu.SemaphoreType.DMA((BATCHES, total)),
            pltpu.SemaphoreType.DMA((BATCHES, n_mem, owners)),
            pltpu.SemaphoreType.DMA((total,)),
            pltpu.SemaphoreType.DMA((1, c_owners)),
        ],
        compiler_params=pltpu.CompilerParams(
            collective_id=0, has_side_effects=True, vmem_limit_bytes=40 * 1024 * 1024
        ),
    )(
        state,
        centers[None, :],
        half_width[None, :],
        radius[None, :],
        order[None, :],
        obs_var[None, :],
    )


def solution(mesh):
    shape = (mesh.shape["slab"], mesh.shape["mem"], mesh.shape["sub"])
    placed = (P("mem", ("grp", "slab", "sub")), P("grp"), P("grp"), P("grp"), P("grp"), P("grp"))
    return jax.shard_map(
        functools.partial(on_device, shape),
        mesh=mesh,
        in_specs=placed,
        out_specs=P("mem", ("grp", "slab", "sub")),
        check_vma=False,
    )
```

```python
import functools
import math

import jax
import jax.numpy as jnp
from jax import lax
from jax.experimental import pallas as pl
from jax.experimental.pallas import tpu as pltpu
from jax.sharding import PartitionSpec as P

M = 256
P_SIZE = 128
BATCHES = 2
BLOCK = 16
SPLIT = 4
SPLIT_2 = 4

FLOOR = math.exp(-2.0)
F32 = jnp.float32
BF16 = jnp.bfloat16
HIGH = lax.Precision.HIGHEST
LAST = (((1,), (1,)), ((), ()))
FIRST = (((0,), (0,)), ((), ()))


def each(start, stop, body):
    if stop - start <= 16:
        for i in range(start, stop):
            body(i)
    else:

        def step(i, carry):
            body(i)
            return carry

        lax.fori_loop(start, stop, step, 0)


def split3(x):
    high = x.astype(BF16)
    rest = x - high.astype(F32)
    mid = rest.astype(BF16)
    low = (rest - mid.astype(F32)).astype(BF16)
    return high, mid, low


def sweep(work, inv, solved, root, first=0, last=P_SIZE // BLOCK):
    b = BLOCK
    width = work.shape[1] // P_SIZE

    def step(k, carry):
        r0 = pl.multiple_of(k * b, b)
        parts = [work[pl.ds(r0, b), g * P_SIZE : (g + 1) * P_SIZE] for g in range(width)]
        roots = root[pl.ds(r0, b), :]
        rolled = pltpu.roll(parts[0], lax.rem(P_SIZE - r0, P_SIZE), 1)
        cols = [jnp.broadcast_to(rolled[:, j : j + 1], (b, P_SIZE)) for j in range(b)]
        row_id = lax.broadcasted_iota(jnp.int32, (b, P_SIZE), 0)
        for j in range(b):
            pivot = cols[j][j : j + 1, :]
            scale = lax.rsqrt(pivot)
            scale_m = 1.0 / (pivot * scale + roots[j : j + 1, :])
            column = jnp.where(row_id > j, cols[j] * scale, 0.0)
            for i in range(j + 1, b):
                cols[i] = cols[i] - column * column[i : i + 1, :]
            for g in range(width):
                row = parts[g][j : j + 1, :] * (scale if g < 2 else scale_m)
                parts[g] = jnp.where(row_id == j, row, parts[g] - column * row)
        inv[pl.ds(r0, b), :] = parts[1]
        for g in range(2, width):
            solved[pl.ds(r0, b), (g - 2) * P_SIZE : (g - 1) * P_SIZE] = parts[g]
        pieces = [split3(x) for x in parts]
        h, m, l = pieces[0]
        left = jnp.concatenate([h, h, m, h, m, l], axis=0)
        h, m, l = (jnp.concatenate([x[n] for x in pieces], axis=1) for n in range(3))
        right = jnp.concatenate([h, m, h, l, m, h], axis=0)
        work[...] -= lax.dot_general(left, right, FIRST, preferred_element_type=F32)
        return carry

    lax.fori_loop(first, last, step, 0)


def kernel(
    shape,
    state_hbm, cen_hbm, half_hbm, rad_hbm, order_hbm, var_hbm,
    out,
    state, cen, half, rad, order, var,
    e_all, foot, tap, tap1, col_c, col_r, var_b, root_b, work, inv, solved, wts,
    part, rs, ag, cpart, crs, cag,
    in_s, e_ss, e_rs, t_ss, t_rs, rs_ss, rs_rs, crs_ss, crs_rs, ag_ss, ag_rs, cag_ss, cag_rs,
):
    n_slab, n_mem, n_sub = shape
    n = n_slab * n_sub
    total = n * n_mem
    own, rows = state.shape
    part_rows = rows // n_mem

    mi = lax.axis_index("mem")
    me = lax.axis_index("slab") * n_sub + lax.axis_index("sub")

    def peer(red, mem):
        return {"slab": lax.div(red, n_sub), "sub": lax.rem(red, n_sub), "mem": mem}

    def peer_of(off):
        red = lax.rem(me + lax.rem(off, n), n)
        mem = lax.rem(mi + lax.div(off, n), n_mem)
        return red, mem

    inputs = [
        pltpu.make_async_copy(a, b, in_s.at[i])
        for i, (a, b) in enumerate(
            zip(
                (state_hbm, cen_hbm, half_hbm, rad_hbm, order_hbm, var_hbm),
                (state, cen, half, rad, order, var),
            )
        )
    ]
    for copy in inputs[1:] + inputs[:1]:
        copy.start()

    barrier = pltpu.get_barrier_semaphore()

    def greet(off):
        red, mem = peer_of(off)
        pl.semaphore_signal(
            barrier, inc=1, device_id=peer(red, mem), device_id_type=pl.DeviceIdType.MESH
        )

    each(1, total, greet)
    for copy in inputs[1:]:
        copy.wait()

    n_obs = BATCHES * P_SIZE
    picked = jnp.broadcast_to(order[...].astype(F32), (P_SIZE, n_obs)).T.astype(jnp.int32)
    lane = lax.broadcasted_iota(jnp.int32, (n_obs, P_SIZE), 1)
    masks = [picked == lane + h * P_SIZE for h in range(BATCHES)]

    def pick(ref):
        value = ref[...].astype(F32)
        chosen = 0.0
        for h in range(BATCHES):
            chosen = chosen + jnp.where(masks[h], value[:, h * P_SIZE : (h + 1) * P_SIZE], 0.0)
        return jnp.sum(chosen, axis=1, keepdims=True)

    center = pick(cen) - (me * rows).astype(F32)
    width = pick(half)
    variance = pick(var)
    col_c[...] = jnp.broadcast_to(center, (n_obs, P_SIZE))
    col_r[...] = jnp.broadcast_to(1.0 / pick(rad), (n_obs, P_SIZE))
    var_b[...] = jnp.broadcast_to(variance, (n_obs, P_SIZE))
    root_b[...] = jnp.broadcast_to(jnp.sqrt(variance), (n_obs, P_SIZE))
    steep = -2.0 / (width * width)
    height = 1.0 / jnp.sqrt(width)

    def rows_of(mem):
        return pl.ds(pl.multiple_of(mem * part_rows, part_rows), part_rows)

    my_rows = rows_of(mi)

    def e_copy(off):
        to = lax.rem(mi + off, n_mem)
        return pltpu.make_async_remote_copy(
            src_ref=state_hbm.at[:, rows_of(to)],
            dst_ref=e_all.at[mi],
            send_sem=e_ss.at[off],
            recv_sem=e_rs.at[mi],
            device_id=peer(me, to),
            device_id_type=pl.DeviceIdType.MESH,
        )

    def foot_tile(t, carry):
        at = pl.multiple_of(t * 256, 256)
        row = lax.broadcasted_iota(jnp.int32, (n_obs, 256), 1) + at
        distance = row.astype(F32) - center
        shape_f = jnp.maximum(jnp.exp(distance * distance * steep) - FLOOR, 0.0) * height
        foot[:, pl.ds(at, 256)] = shape_f.astype(BF16)
        return carry

    lax.fori_loop(0, rows // 256, foot_tile, 0)
    inputs[0].wait()
    sums = lax.dot_general(foot[...], state[...], LAST, preferred_element_type=F32)
    for b in range(BATCHES):
        part[b] = sums[b * P_SIZE : (b + 1) * P_SIZE, :].reshape(part.shape[1:])

    class Sum:
        def __init__(self, size, index, device, source, target, result, everyone, sems):
            self.size, self.index, self.device = size, index, device
            self.source, self.target, self.result, self.everyone = source, target, result, everyone
            self.rs_ss, self.rs_rs, self.ag_ss, self.ag_rs = sems
            self.owners = source.shape[0]
            self.stride = size // self.owners
            self.mine = lax.div(index, self.stride)

        def remote(self, src, dst, send, recv, device):
            return pltpu.make_async_remote_copy(
                src_ref=src, dst_ref=dst, send_sem=send, recv_sem=recv,
                device_id=device, device_id_type=pl.DeviceIdType.MESH,
            )

        def if_owner(self, body, owner=True):
            if self.stride == 1:
                if owner:
                    body()
            else:
                pl.when((lax.rem(self.index, self.stride) == 0) == owner)(body)

        def out_copy(self, off):
            o = lax.rem(self.mine + off, self.owners)
            return self.remote(
                self.source.at[o], self.target.at[self.index],
                self.rs_ss.at[off], self.rs_rs.at[self.index], self.device(o * self.stride),
            )

        def start(self):
            each(1, self.owners, lambda off: self.out_copy(off).start())
            self.if_owner(lambda: self.out_copy(0).start(), False)

        def gather_copy(self, off):
            block = self.result(mi, self.mine)
            return self.remote(
                block, block, self.ag_ss.at[off],
                self.ag_rs.at[mi if self.everyone else 0, self.mine], peer(*peer_of(off)),
            )

        def finish(self):
            def body():
                for off in range(1, self.size) if self.size <= 16 else ():
                    self.arrived(lax.rem(self.index + off, self.size))
                block = self.result(mi, self.mine)
                value = self.source[self.mine]
                if self.size <= 16:
                    for off in range(1, self.size):
                        value = value + self.target[lax.rem(self.index + off, self.size)]
                    block[...] = value
                else:
                    block[...] = value

                    def add(off):
                        src = lax.rem(self.index + off, self.size)
                        self.arrived(src)
                        block[...] += self.target[src]

                    each(1, self.size, add)
                each(1, total, lambda off: self.gather_copy(off).start())

            self.if_owner(body)

        def arrived(self, src):
            self.remote(
                self.source.at[0], self.target.at[src], self.rs_ss.at[0], self.rs_rs.at[src],
                self.device(src),
            ).wait_recv()

        def gather(self):
            mems = n_mem if self.everyone else 1

            def one(q):
                o = lax.rem(self.mine + lax.rem(q, self.owners), self.owners)
                mem = lax.rem(mi + lax.div(q, self.owners), n_mem)
                block = self.result(mem, o)
                self.remote(
                    block, block, self.ag_ss.at[0],
                    self.ag_rs.at[mem if self.everyone else 0, o],
                    self.device(o * self.stride),
                ).wait_recv()

            each(1, mems * self.owners, one)
            self.if_owner(lambda: one(0), False)

        def sent(self):
            each(1, self.owners, lambda off: self.out_copy(off).wait_send())
            self.if_owner(lambda: self.out_copy(0).wait_send(), False)
            self.if_owner(
                lambda: each(1, total, lambda off: self.gather_copy(off).wait_send())
            )

    projections = [
        Sum(
            n, me, lambda i: peer(i, mi), part.at[b], rs.at[b],
            lambda mem, o, b=b: ag.at[b, mem, o], True,
            (rs_ss.at[b], rs_rs.at[b], ag_ss.at[b], ag_rs.at[b]),
        )
        for b in range(BATCHES)
    ]
    changes = Sum(
        total, mi * n + me, lambda i: peer(lax.rem(i, n), lax.div(i, n)), cpart, crs,
        lambda mem, o: cag.at[o], False, (crs_ss, crs_rs, cag_ss, cag_rs),
    )
    pl.semaphore_wait(barrier, total - 1)
    for x in projections:
        x.start()
    each(1, n_mem, lambda off: e_copy(off).start())
    e_all[mi] = state[:, my_rows]
    projections[0].finish()

    def slot(b, s):
        return ag[b, s].reshape(P_SIZE, own)

    def load_work(columns, b):
        cov = 0.0
        for s in range(n_mem):
            cov = cov + lax.dot_general(
                columns[s], columns[s], LAST, precision=HIGH, preferred_element_type=F32
            )
        r = lax.broadcasted_iota(jnp.int32, (P_SIZE, P_SIZE), 0)
        eye = r == lax.broadcasted_iota(jnp.int32, (P_SIZE, P_SIZE), 1)
        v = var_b[b * P_SIZE : (b + 1) * P_SIZE, :]
        work[:, :P_SIZE] = cov * (1.0 / (M - 1)) + jnp.where(eye, v, 0.0)
        work[:, P_SIZE : 2 * P_SIZE] = jnp.where(eye, 1.0, 0.0)
        for s in range(n_mem):
            lo = 2 * P_SIZE + s * own
            work[:, lo : lo + own] = columns[s]

    def taper(b):
        lo = b * P_SIZE
        row = lax.broadcasted_iota(jnp.int32, (P_SIZE, part_rows), 1) + mi * part_rows
        c = jnp.concatenate([col_c[lo : lo + P_SIZE, :]] * (part_rows // P_SIZE), axis=1)
        r = jnp.concatenate([col_r[lo : lo + P_SIZE, :]] * (part_rows // P_SIZE), axis=1)
        near = jnp.maximum(1.0 - jnp.abs(row.astype(F32) - c) * r, 0.0)
        return near * near * (1.0 / (M - 1))

    def t_copy(x, ref, off):
        return pltpu.make_async_remote_copy(
            src_ref=ref.at[mi],
            dst_ref=ref.at[mi],
            send_sem=t_ss.at[x, off],
            recv_sem=t_rs.at[x, mi],
            device_id=peer(me, lax.rem(mi + off, n_mem)),
            device_id_type=pl.DeviceIdType.MESH,
        )

    def t_wait(x, ref, off):
        src = lax.rem(mi + off, n_mem)
        pltpu.make_async_remote_copy(
            src_ref=ref.at[src],
            dst_ref=ref.at[src],
            send_sem=t_ss.at[x, 0],
            recv_sem=t_rs.at[x, src],
            device_id=peer(me, src),
            device_id_type=pl.DeviceIdType.MESH,
        ).wait_recv()

    projections[0].gather()
    first = [slot(0, s) for s in range(n_mem)]
    first_b = [x.astype(BF16) for x in first]

    def e_wait(off):
        src = lax.rem(mi + off, n_mem)
        pltpu.make_async_remote_copy(
            src_ref=e_all.at[src],
            dst_ref=e_all.at[src],
            send_sem=e_ss.at[0],
            recv_sem=e_rs.at[src],
            device_id=peer(me, src),
            device_id_type=pl.DeviceIdType.MESH,
        ).wait_recv()

    each(1, n_mem, e_wait)

    cross = 0.0
    for s in range(n_mem):
        cross = cross + jnp.dot(first_b[s], e_all[s], preferred_element_type=F32)
    before = (taper(0) * cross).astype(BF16)
    tap[mi] = before
    change = lax.dot_general(
        foot[P_SIZE : 2 * P_SIZE, my_rows], before, LAST, preferred_element_type=F32
    )
    cpart[...] = change.reshape(cpart.shape)
    changes.start()
    projections[1].finish()

    load_work(first, 0)
    sweep(work, inv, solved, root_b.at[pl.ds(0, P_SIZE)], 0, SPLIT)
    changes.finish()
    each(1, n_mem, lambda off: t_copy(0, tap, off).start())
    sweep(work, inv, solved, root_b.at[pl.ds(0, P_SIZE)], SPLIT)

    def weights():
        return lax.dot_general(
            solved[...], inv[...], FIRST, precision=HIGH, preferred_element_type=F32
        )

    wts[...] = weights().astype(BF16)

    projections[1].gather()
    changes.gather()
    c_full = cag[...].reshape(P_SIZE, P_SIZE)
    second = []
    for s in range(n_mem):
        moved = lax.dot_general(
            c_full,
            wts[s * own : (s + 1) * own, :].astype(F32),
            LAST,
            precision=HIGH,
            preferred_element_type=F32,
        )
        second.append(slot(1, s) - moved)
    second_b = [x.astype(BF16) for x in second]

    before = tap[mi]
    cross = 0.0
    for s in range(n_mem):
        moved = jnp.dot(wts[s * own : (s + 1) * own, :], before, preferred_element_type=F32)
        now = (e_all[s].astype(F32) - moved).astype(BF16)
        cross = cross + jnp.dot(second_b[s], now, preferred_element_type=F32)
    tap1[mi] = (taper(1) * cross).astype(BF16)
    each(1, n_mem, lambda off: t_copy(1, tap1, off).start())

    load_work(second, 1)
    own_w = wts[pl.ds(pl.multiple_of(mi * own, own), own), :]
    sweep(work, inv, solved, root_b.at[pl.ds(P_SIZE, P_SIZE)], 0, SPLIT_2)
    each(1, n_mem, lambda off: t_wait(0, tap, off))
    for mem in range(n_mem):
        at = slice(mem * part_rows, (mem + 1) * part_rows)
        moved = jnp.dot(own_w, tap[mem], preferred_element_type=F32)
        out[:, at] = (state[:, at].astype(F32) - moved).astype(BF16)
    sweep(work, inv, solved, root_b.at[pl.ds(P_SIZE, P_SIZE)], SPLIT_2)
    wts[...] = weights().astype(BF16)
    own_w = wts[pl.ds(pl.multiple_of(mi * own, own), own), :]

    for off in range(n_mem):
        if off:
            t_wait(1, tap1, off)
        mem = lax.rem(mi + off, n_mem)
        at = rows_of(mem)
        moved = jnp.dot(own_w, tap1[mem], preferred_element_type=F32)
        out[:, at] = (out[:, at].astype(F32) - moved).astype(BF16)

    each(1, n_mem, lambda off: e_copy(off).wait_send())
    for x, ref in enumerate((tap, tap1)):
        each(1, n_mem, lambda off: t_copy(x, ref, off).wait_send())
    for x in projections + [changes]:
        x.sent()


def on_device(shape, state, centers, half_width, radius, order, obs_var):
    n_slab, n_mem, n_sub = shape
    own, rows = state.shape
    n = n_slab * n_sub
    total = n * n_mem
    owners = min(n, 4)
    chunk = P_SIZE // owners
    c_owners = min(total, 8)
    c_chunk = P_SIZE // c_owners
    n_obs = BATCHES * P_SIZE
    part_rows = rows // n_mem
    hbm = pl.BlockSpec(memory_space=pltpu.HBM)
    vmem = pl.BlockSpec(memory_space=pltpu.VMEM)
    return pl.pallas_call(
        functools.partial(kernel, shape),
        out_shape=jax.ShapeDtypeStruct((own, rows), BF16),
        in_specs=[hbm] * 6,
        out_specs=vmem,
        scratch_shapes=[
            pltpu.VMEM((own, rows), BF16),
            pltpu.VMEM((1, n_obs), jnp.int32),
            pltpu.VMEM((1, n_obs), jnp.int32),
            pltpu.VMEM((1, n_obs), jnp.int32),
            pltpu.VMEM((1, n_obs), jnp.int32),
            pltpu.VMEM((1, n_obs), F32),
            pltpu.VMEM((n_mem, own, part_rows), BF16),
            pltpu.VMEM((n_obs, rows), BF16),
            pltpu.VMEM((n_mem, P_SIZE, part_rows), BF16),
            pltpu.VMEM((n_mem, P_SIZE, part_rows), BF16),
            pltpu.VMEM((n_obs, P_SIZE), F32),
            pltpu.VMEM((n_obs, P_SIZE), F32),
            pltpu.VMEM((n_obs, P_SIZE), F32),
            pltpu.VMEM((n_obs, P_SIZE), F32),
            pltpu.VMEM((P_SIZE, 2 * P_SIZE + M), F32),
            pltpu.VMEM((P_SIZE, P_SIZE), F32),
            pltpu.VMEM((P_SIZE, M), F32),
            pltpu.VMEM((M, P_SIZE), BF16),
            pltpu.VMEM((BATCHES, owners, chunk, own), F32),
            pltpu.VMEM((BATCHES, n, chunk, own), F32),
            pltpu.VMEM((BATCHES, n_mem, owners, chunk, own), F32),
            pltpu.VMEM((c_owners, c_chunk, P_SIZE), F32),
            pltpu.VMEM((total, c_chunk, P_SIZE), F32),
            pltpu.VMEM((c_owners, c_chunk, P_SIZE), F32),
            pltpu.SemaphoreType.DMA((6,)),
            pltpu.SemaphoreType.DMA((n_mem,)),
            pltpu.SemaphoreType.DMA((n_mem,)),
            pltpu.SemaphoreType.DMA((BATCHES, n_mem)),
            pltpu.SemaphoreType.DMA((BATCHES, n_mem)),
            pltpu.SemaphoreType.DMA((BATCHES, owners)),
            pltpu.SemaphoreType.DMA((BATCHES, n)),
            pltpu.SemaphoreType.DMA((c_owners,)),
            pltpu.SemaphoreType.DMA((total,)),
            pltpu.SemaphoreType.DMA((BATCHES, total)),
            pltpu.SemaphoreType.DMA((BATCHES, n_mem, owners)),
            pltpu.SemaphoreType.DMA((total,)),
            pltpu.SemaphoreType.DMA((1, c_owners)),
        ],
        compiler_params=pltpu.CompilerParams(
            collective_id=0, has_side_effects=True, vmem_limit_bytes=40 * 1024 * 1024
        ),
    )(
        state,
        centers[None, :],
        half_width[None, :],
        radius[None, :],
        order[None, :],
        obs_var[None, :],
    )


def solution(mesh):
    shape = (mesh.shape["slab"], mesh.shape["mem"], mesh.shape["sub"])
    placed = (P("mem", ("grp", "slab", "sub")), P("grp"), P("grp"), P("grp"), P("grp"), P("grp"))
    return jax.shard_map(
        functools.partial(on_device, shape),
        mesh=mesh,
        in_specs=placed,
        out_specs=P("mem", ("grp", "slab", "sub")),
        check_vma=False,
    )
```
